128 devices in a mesh: blk: 32 (over x, z_hi, y), rep: 4 (over z_lo, core).
Axes of the slice: x: 4, y: 4, z: 4 (z_hi: 2, z_lo: 2; z = z_hi * 2 + z_lo), core: 2. Of those that a mesh axis runs over, the one named last changes fastest.
Arguments:
- generated: float32 [8192, 1024], P(('blk', 'rep')), may hold values from -6 to 6
- real_bank: float32 [65536, 1024], P(('blk', 'rep')), may hold values from -6 to 6
- subset_rows: int32 [32768], P(('blk', 'rep')), may hold values from 0 to 511
Outputs:
- gradient: float32 [8192, 1024], P(('blk', 'rep'))
The draws below stay inside these ranges and needn't reach their ends.
All inputs are finite; a program needn't handle non-finite values.
Results may differ from the reference program's by a relative error of at most 0.0003.
Values sent between devices are 32-bit elements; how exact they have to be, the bound alone decides.
No kernel may reach another device: no remote copies, remote signals or barrier semaphores. Data moves between devices by JAX's collectives and lax.ppermute only.
A program may use at most 128 MiB of HBM per device.

```python
import math
import jax
import jax.numpy as jnp
from jax import lax

D = 1024
REAL_DEV = 256
BANK_DEV = 512
M = 8192
R = 32768
BANK = 65536


class_count = 64


latent_count = 8


def class_centres(key, latent_scale, private_scale):
    direction_key = jax.random.fold_in(key, 101)
    position_key = jax.random.fold_in(key, 102)
    private_key = jax.random.fold_in(key, 103)
    directions = jnp.clip(jax.random.normal(direction_key, (latent_count, D), jnp.float32), -4.0, 4.0)
    positions = jnp.clip(jax.random.normal(position_key, (class_count, latent_count), jnp.float32), -4.0, 4.0)
    centres = private_scale * jnp.clip(jax.random.normal(private_key, (class_count, D), jnp.float32), -4.0, 4.0)
    for column in range(latent_count):
        centres = centres + latent_scale * positions[:, column:column + 1] * directions[column:column + 1, :]
    return centres


def draw_generated(key, part):
    centres = class_centres(key, 0.32, 0.7)
    key = jax.random.fold_in(key, 7)
    label_key = jax.random.fold_in(key, 1)
    noise_key = jax.random.fold_in(key, 2)
    labels = jax.random.randint(label_key, (M,), 0, class_count)
    picked = jnp.take(centres, labels, axis=0)
    noise = jnp.clip(jax.random.normal(noise_key, (M, D), jnp.float32), -4.0, 4.0)
    rows = 0.9 * picked + 0.55 * noise
    return jnp.clip(rows, -6.0, 6.0)


def draw_real_bank(key, part):
    centres = class_centres(key, 0.32, 0.7)
    key = jax.random.fold_in(key, 9)
    label_key = jax.random.fold_in(key, 1)
    noise_key = jax.random.fold_in(key, 2)
    labels = jax.random.randint(label_key, (BANK,), 0, class_count)
    picked = jnp.take(centres, labels, axis=0)
    noise = jnp.clip(jax.random.normal(noise_key, (BANK, D), jnp.float32), -4.0, 4.0)
    rows = picked + 0.7 * noise
    return jnp.clip(rows, -6.0, 6.0)


def place_ends(array, own_key, low, high):
    shape = array.shape
    spot = [jax.random.randint(jax.random.fold_in(own_key, axis), (), 0, shape[axis]) for axis in range(len(shape))]
    array = array.at[tuple(spot)].set(low)
    longest = shape.index(max(shape))
    spot[longest] = (spot[longest] + 1) % shape[longest]
    return array.at[tuple(spot)].set(high)


def setup_inputs(seed: int = 0) -> dict:
    streams_of = jax.random.split(jax.random.key(seed), 4)
    return {
        "generated": draw_generated(jax.random.fold_in(streams_of[3], 71), 0),
        "real_bank": draw_real_bank(jax.random.fold_in(streams_of[3], 71), 0),
        "subset_rows": place_ends(jax.random.randint(streams_of[2], (R,), 0, BANK_DEV), jax.random.fold_in(streams_of[2], 1), 0, BANK_DEV - 1).astype(jnp.int32),
    }


BANDS = (0.5, 1.0, 2.0)


def kernel_weight(dist, width):
    total = jnp.zeros_like(dist)
    for factor in BANDS:
        total = total + jnp.exp(-dist / (2.0 * factor * width)) / factor
    return total


def pair_parts(rows, others):
    row_norms = jnp.sum(rows * rows, axis=1)
    other_norms = jnp.sum(others * others, axis=1)
    inner = jnp.dot(rows, others.T, precision=lax.Precision.HIGHEST, preferred_element_type=jnp.float32)
    dist = jnp.maximum(row_norms[:, None] + other_norms[None, :] - 2.0 * inner, 0.0)
    weights = kernel_weight(dist, float(rows.shape[1]))
    weighted = jnp.dot(weights, others, precision=lax.Precision.HIGHEST, preferred_element_type=jnp.float32)
    return jnp.sum(weights, axis=1)[:, None] * rows - weighted


def reference(generated, real_bank, subset_rows):
    owner = jnp.arange(R, dtype=jnp.int32) // REAL_DEV
    real = real_bank[owner * BANK_DEV + subset_rows]
    step_rows = math.gcd(M, 512)
    blocks = generated.reshape(M // step_rows, step_rows, D)

    def one_block(rows):
        return pair_parts(rows, generated) / M - pair_parts(rows, real) / R

    return lax.map(one_block, blocks).reshape(M, D)
```

```python
import functools
import math

import jax
import jax.numpy as jnp
from jax import lax
from jax.experimental import pallas as pl
from jax.experimental.pallas import tpu as pltpu
from jax.sharding import PartitionSpec as P

AXES = ("blk", "rep")
SIDE = 4


def ring(axis):
    pairs = []
    for x in range(SIDE):
        for y in range(SIDE):
            for z in range(SIDE):
                for core in range(2):
                    step = 1 if core == 0 else -1
                    to = {"x": x, "y": y, "z": z}
                    to[axis] = (to[axis] + step) % SIDE
                    pairs.append((place(x, y, z, core), place(to["x"], to["y"], to["z"], core)))
    return pairs


def place(x, y, z, core):
    blk = (x * 2 + z // 2) * SIDE + y
    return blk * 4 + (z % 2) * 2 + core


RINGS = {axis: ring(axis) for axis in "xyz"}
SWAP = [(d, d ^ 1) for d in range(2 * SIDE**3)]


def hop(v, axis):
    return lax.ppermute(v, AXES, RINGS[axis])


def swap(v):
    return lax.ppermute(v, AXES, SWAP)


def dot_t(a, b):
    return lax.dot_general(a, b, (((1,), (1,)), ((), ())), preferred_element_type=jnp.float32)


def pair_kernel(n_real, n_gen, first, last, scale, *refs):
    width = refs[0].shape[1]
    kappa = math.log2(math.e) / (4.0 * width)
    rows_refs, refs = refs[:2], refs[2:]
    real_refs, refs = refs[:n_real], refs[n_real:]
    gen_refs, refs = refs[:n_gen], refs[n_gen:]
    if not first:
        (acc_in, sum_in), refs = refs[:2], refs[2:]
    rows = jnp.concatenate([r[...] for r in rows_refs], axis=0)
    row_norms = jnp.sum(rows * rows, axis=1, keepdims=True) * kappa
    rows_b = (rows * (2.0 * kappa)).astype(jnp.bfloat16)

    def weights(others, a, b, c):
        norms = jnp.sum(others * others, axis=1, keepdims=True) * kappa
        norms = jnp.transpose(jnp.broadcast_to(norms, (norms.shape[0], 128)))[:1]
        others_b = others.astype(jnp.bfloat16)
        power = jnp.minimum(dot_t(rows_b, others_b) - row_norms - norms, 0.0)
        e = jnp.exp2(power)
        e2 = e * e
        return a * e + e2 * (b + c * e2), others_b

    def lanes(w):
        return sum(w[:, k:k + 128] for k in range(0, w.shape[1], 128))

    acc = None if first else acc_in[...]
    sums = None if first else sum_in[...]

    def add(total, part):
        return part if total is None else total + part

    for k in range(0, n_real, 2):
        others = jnp.concatenate([r[...] for r in real_refs[k:k + 2]], axis=0)
        w, others_b = weights(others, -0.5, -1.0, -2.0)
        sums = add(sums, lanes(w))
        acc = add(acc, jnp.dot(w.astype(jnp.bfloat16), others_b, preferred_element_type=jnp.float32))
    for k in range(0, n_gen, 4):
        others = jnp.concatenate([r[...] for r in gen_refs[k:k + 4]], axis=0)
        w, others_b = weights(others, 0.5 * scale, 1.0 * scale, 2.0 * scale)
        sums = add(sums, lanes(w))
        w_hi = w.astype(jnp.bfloat16)
        w_lo = (w - w_hi.astype(jnp.float32)).astype(jnp.bfloat16)
        others_lo = (others - others_b.astype(jnp.float32)).astype(jnp.bfloat16)
        acc = add(acc, jnp.dot(w_hi, others_b, preferred_element_type=jnp.float32))
        acc = acc + jnp.dot(w_lo, others_b, preferred_element_type=jnp.float32)
        acc = acc + jnp.dot(w_hi, others_lo, preferred_element_type=jnp.float32)
    if not last:
        acc_out, sum_out = refs
        acc_out[...] = acc
        sum_out[...] = sums
    else:
        total = jnp.sum(sums, axis=1, keepdims=True)
        out = (total * rows - acc) * last
        half = out.shape[0] // 2
        refs[0][...] = out[:half]
        refs[1][...] = out[half:]


def pairs(rows, reals, gens, state, last, scale):
    count, width = 2 * rows[0].shape[0], rows[0].shape[1]
    f32 = jnp.float32
    if last:
        out_shape = (jax.ShapeDtypeStruct((count // 2, width), f32),) * 2
    else:
        out_shape = (jax.ShapeDtypeStruct((count, width), f32), jax.ShapeDtypeStruct((count, 128), f32))
    operands = [*rows, *reals, *gens, *(state or ())]
    aliases = {}
    if state and not last:
        aliases = {len(operands) - 2: 0, len(operands) - 1: 1}
    return pl.pallas_call(
        functools.partial(pair_kernel, len(reals), len(gens), state is None, last, scale),
        out_shape=out_shape,
        in_specs=[pl.BlockSpec(memory_space=pltpu.VMEM)] * len(operands),
        out_specs=(pl.BlockSpec(memory_space=pltpu.VMEM),) * len(out_shape),
        input_output_aliases=aliases,
        compiler_params=pltpu.CompilerParams(vmem_limit_bytes=40 * 2**20),
    )(*operands)


def around(v, axis):
    out = [v]
    for _ in range(SIDE - 1):
        out.append(hop(out[-1], axis))
    return out


def on_device(generated, real_bank, subset_rows):
    devices = lax.axis_size("blk") * lax.axis_size("rep")
    total_gen = generated.shape[0] * devices
    total_real = subset_rows.shape[0] * devices
    n = generated.shape[0]

    real = real_bank.at[subset_rows].get(mode="promise_in_bounds")
    half = real.shape[0] // 2

    one = jnp.concatenate(around(generated[: n // 2], "x"), axis=0)
    two = jnp.concatenate(around(generated[n // 2 :], "y"), axis=0)
    rows = list(zip(around(one, "y"), around(two, "x")))

    gens = around(generated, "z")
    reals_a = around(real[:half], "z")
    reals_b = around(real[half:], "z")
    gens = [(v, swap(v)) for v in gens]
    reals = [(a, swap(a), b, swap(b)) for a, b in zip(reals_a, reals_b)]
    gens = [v for pair in gens for v in pair]

    scale = total_real // total_gen
    parts = [None] * SIDE
    states = [None] * SIDE
    for t in range(SIDE):
        states[t] = pairs(rows[t], reals[0] + reals[1], (), None, None, scale)
    for t in range(SIDE):
        states[t] = pairs(rows[t], reals[2], gens, states[t], None, scale)
    for t in (1, 2, 3, 0):
        parts[t] = pairs(rows[t], reals[3], (), states[t], 1.0 / total_real, scale)

    def scatter(parts, axis):
        total = parts[1]
        for t in (2, 3, 0):
            total = hop(total, axis) + parts[t]
        return total

    one = scatter([p[0] for p in parts], "y")
    two = scatter([p[1] for p in parts], "x")
    one = scatter([one[k : k + n // 2] for k in range(0, 2 * n, n // 2)], "x")
    two = scatter([two[k : k + n // 2] for k in range(0, 2 * n, n // 2)], "y")
    return jnp.concatenate([one, two], axis=0)


def solution(mesh):
    in_specs = (P(AXES, None), P(AXES, None), P(AXES))
    return jax.shard_map(on_device, mesh=mesh, in_specs=in_specs, out_specs=P(AXES, None), check_vma=False)
```

```python
import functools
import math

import jax
import jax.numpy as jnp
from jax import lax
from jax.experimental import pallas as pl
from jax.experimental.pallas import tpu as pltpu
from jax.sharding import PartitionSpec as P

AXES = ("blk", "rep")
SIDE = 4


def place(x, y, z, core):
    blk = (x * 2 + z // 2) * SIDE + y
    return blk * 4 + (z % 2) * 2 + core


def partners(axes, step):
    pairs = []
    for x in range(SIDE):
        for y in range(SIDE):
            for z in range(SIDE):
                for core in range(2):
                    to = {"x": x, "y": y, "z": z}
                    at = to[axes[core]]
                    if step == "both" or (step == "near") == (core == 0):
                        at = at ^ 1
                    if step == "both" or (step == "near") == (core == 1):
                        at = SIDE - 1 - at
                    to[axes[core]] = at
                    pairs.append((place(x, y, z, core), place(to["x"], to["y"], to["z"], core)))
    return pairs


STEPS = {(axes, step): partners(axes, step) for axes in ("xy", "yx", "zz") for step in ("near", "far", "both")}
SWAP = [(d, d ^ 1) for d in range(2 * SIDE**3)]


def move(v, axes, step):
    return lax.ppermute(v, AXES, STEPS[axes, step])


def swap(v):
    return lax.ppermute(v, AXES, SWAP)


def dot_t(a, b):
    return lax.dot_general(a, b, (((1,), (1,)), ((), ())), preferred_element_type=jnp.float32)


def lanes(w):
    return sum(w[:, k : k + 128] for k in range(0, w.shape[1], 128))


def pair_kernel(counts, spans, fresh, last, scale, *refs):
    take = iter(refs)
    n_batch = len(counts)
    rows_refs = [[next(take) for _ in range(count)] for count in counts]
    other_refs = [next(take) for _ in spans]
    state_in = [None if new else (next(take), next(take)) for new in fresh]
    state_out = [[next(take) for _ in range(count if last else 2)] for count in counts]
    others_b, others_norms = take
    width = rows_refs[0][0].shape[1]
    kappa = math.log2(math.e) / (4.0 * width)

    def norms_of(others):
        norms = jnp.sum(others * others, axis=1, keepdims=True) * kappa
        return jnp.transpose(jnp.broadcast_to(norms, (norms.shape[0], 128)))[:8]

    gens, reals = [], []
    for ref, span in zip(other_refs, spans):
        if span:
            gens.append(ref[:span])
        reals.append(ref[span:])
    reals = jnp.concatenate(reals, axis=0)
    n_real = reals.shape[0]
    others_norms[:, :n_real] = norms_of(reals)
    others_b[:n_real] = reals.astype(jnp.bfloat16)
    n_gen = sum(spans)
    end = n_real + n_gen
    if n_gen:
        gens = jnp.concatenate(gens, axis=0)
        others_norms[:, n_real:] = norms_of(gens)
        high = gens.astype(jnp.bfloat16)
        others_b[n_real:end] = high
        others_b[end : end + n_gen] = (gens - high.astype(jnp.float32)).astype(jnp.bfloat16)
        others_b[end + n_gen :] = high

    for k in range(n_batch):
        rows = jnp.concatenate([r[...] for r in rows_refs[k]], axis=0)
        row_norms = jnp.sum(rows * rows, axis=1, keepdims=True) * kappa
        rows_b = (rows * (2.0 * kappa)).astype(jnp.bfloat16)

        def weights(at, to, factor):
            power = jnp.minimum(dot_t(rows_b, others_b[at:to]) - row_norms - others_norms[:1, at:to], 0.0)
            e = jnp.exp2(power)
            e2 = e * e
            return (0.5 * factor) * e + e2 * (factor + (2.0 * factor) * e2)

        acc, sums = (0.0, 0.0) if fresh[k] else (state_in[k][0][...], state_in[k][1][...])
        w = weights(0, n_real, -1.0)
        sums = sums + lanes(w)
        w = [w.astype(jnp.bfloat16)]
        if n_gen:
            w_gen = weights(n_real, end, float(scale))
            sums = sums + lanes(w_gen)
            w_hi = w_gen.astype(jnp.bfloat16)
            w += [w_hi, w_hi, (w_gen - w_hi.astype(jnp.float32)).astype(jnp.bfloat16)]
        w = jnp.concatenate(w, axis=1)
        acc = acc + jnp.dot(w, others_b[...], preferred_element_type=jnp.float32)
        if last:
            total = jnp.sum(sums, axis=1, keepdims=True)
            out = (total * rows - acc) * last
            at = 0
            for half in state_out[k]:
                half[...] = out[at : at + half.shape[0]]
                at += half.shape[0]
        else:
            state_out[k][0][...] = acc
            state_out[k][1][...] = sums


def pairs(rows, others, spans, states, last, scale):
    count, width = sum(v.shape[0] for v in rows[0]), rows[0][0].shape[1]
    f32, bf16 = jnp.float32, jnp.bfloat16
    if last:
        shapes = [[jax.ShapeDtypeStruct(v.shape, f32) for v in batch] for batch in rows]
    else:
        shapes = [[jax.ShapeDtypeStruct((count, width), f32), jax.ShapeDtypeStruct((count, 128), f32)] for _ in rows]
    operands = [v for batch in rows for v in batch] + list(others)
    aliases = {}
    for k, state in enumerate(states):
        if state is not None:
            if not last:
                aliases.update({len(operands): 2 * k, len(operands) + 1: 2 * k + 1})
            operands += state
    n_gen = sum(spans)
    n_real = sum(v.shape[0] for v in others) - n_gen
    scratch = [pltpu.VMEM((n_real + 3 * n_gen, width), bf16), pltpu.VMEM((8, n_real + n_gen), f32)]
    n_pairs = count * len(rows) * (n_real + 2 * n_gen)
    vmem = pl.BlockSpec(memory_space=pltpu.VMEM)
    outs = pl.pallas_call(
        functools.partial(pair_kernel, [len(batch) for batch in rows], spans, [s is None for s in states], last, scale),
        out_shape=[v for batch in shapes for v in batch],
        in_specs=[vmem] * len(operands),
        out_specs=[vmem] * sum(len(batch) for batch in shapes),
        scratch_shapes=scratch,
        input_output_aliases=aliases,
        cost_estimate=pl.CostEstimate(
            flops=4 * n_pairs * width, bytes_accessed=4 * width * (n_real + n_gen + 3 * count), transcendentals=n_pairs
        ),
        compiler_params=pltpu.CompilerParams(vmem_limit_bytes=24 * 2**20),
    )(*operands)
    outs = iter(outs)
    return [tuple(next(outs) for _ in batch) for batch in shapes]


def resident(v):
    def copy(v_ref, out_ref):
        out_ref[...] = v_ref[...]

    vmem = pl.BlockSpec(memory_space=pltpu.VMEM)
    return pl.pallas_call(copy, out_shape=jax.ShapeDtypeStruct(v.shape, v.dtype), in_specs=[vmem], out_specs=vmem)(v)


def after(v, *others):
    return lax.optimization_barrier((v, *others))[0]


def resident(v):
    def copy(v_ref, out_ref):
        out_ref[...] = v_ref[...]

    vmem = pl.BlockSpec(memory_space=pltpu.VMEM)
    return pl.pallas_call(copy, out_shape=jax.ShapeDtypeStruct(v.shape, v.dtype), in_specs=[vmem], out_specs=vmem)(v)


def after(v, *others):
    return lax.optimization_barrier((v, *others))[0]


def on_device(generated, real_bank, subset_rows):
    devices = lax.axis_size("blk") * lax.axis_size("rep")
    total_gen = generated.shape[0] * devices
    total_real = subset_rows.shape[0] * devices
    n = generated.shape[0]
    scale = total_real // total_gen
    spans = (n, n)

    generated = resident(generated)
    real = real_bank.at[subset_rows].get(mode="promise_in_bounds", wrap_negative_indices=False)
    own = jnp.concatenate([generated, real], axis=0)
    x_near, x_far = move(own, "zz", "near"), move(own, "zz", "far")

    line = [generated] + [move(generated, "xy", step) for step in ("near", "far", "both")]
    line = jnp.concatenate(line, axis=0)
    half = 2 * n
    own_swapped = swap(after(own, line))
    line_near, line_far = move(line, "yx", "near"), move(line, "yx", "far")

    x_near, x_far, line_near, line_far, own_swapped = lax.optimization_barrier(
        (x_near, x_far, line_near, line_far, own_swapped)
    )
    x_both = move(x_near, "zz", "far")
    x_level = jnp.concatenate([x_near, x_far], axis=0)
    x_level = swap(x_level)
    both = [move(line_near[:half], "yx", "far"), move(line_far[half:], "yx", "near")]
    rows = [[line], [line_near], [line_far], both]
    s = [None] * SIDE
    s[:3] = pairs(rows[:3], (own, own_swapped), spans, s[:3], None, scale)
    x_level, _ = lax.optimization_barrier((x_level, s[:3]))
    count = own.shape[0]
    x_level = (x_near, x_far, x_level[:count], x_level[count:])
    s[:3] = pairs(rows[:3], x_level, spans * 2, s[:3], None, scale)
    x_both, both, _ = lax.optimization_barrier((x_both, both, s[:3]))
    rows[3] = both
    both_two = (x_both, swap(x_both))
    s[3:] = pairs(rows[3:], (own, own_swapped, *x_level), spans * 3, s[3:], None, scale)
    both_two, s = lax.optimization_barrier((both_two, s))
    part = [None] * SIDE
    part[3:] = pairs(rows[3:], both_two, spans, s[3:], 1.0 / total_real, scale)
    s, part[3] = lax.optimization_barrier((s, part[3]))
    part[1:3] = pairs(rows[1:3], both_two, spans, s[1:3], 1.0 / total_real, scale)
    part[:1] = pairs(rows[:1], both_two, spans, s[:1], 1.0 / total_real, scale)

    (total,), (part_near,), (part_far,), both = part
    add_near, add_far = move(both[0], "yx", "far"), move(both[1], "yx", "near")
    near_rest, far_rest = move(part_near[half:], "yx", "near"), move(part_far[:half], "yx", "far")
    add_near, add_far, near_rest, far_rest = lax.optimization_barrier((add_near, add_far, near_rest, far_rest))
    to_near = move(part_near[:half] + add_near, "yx", "near")
    to_far = move(part_far[half:] + add_far, "yx", "far")
    total = jnp.concatenate([total[:half] + to_near + far_rest, total[half:] + near_rest + to_far], axis=0)
    out = total[:n]
    for k, step in enumerate(("near", "far", "both")):
        out = out + move(total[(k + 1) * n : (k + 2) * n], "xy", step)
    return out


def solution(mesh):
    in_specs = (P(AXES, None), P(AXES, None), P(AXES))
    return jax.shard_map(on_device, mesh=mesh, in_specs=in_specs, out_specs=P(AXES, None), check_vma=False)
```

```python
import functools
import math

import jax
import jax.numpy as jnp
from jax import lax
from jax.experimental import pallas as pl
from jax.experimental.pallas import tpu as pltpu
from jax.sharding import PartitionSpec as P

AXES = ("blk", "rep")
SIDE = 4


def place(x, y, z, core):
    blk = (x * 2 + z // 2) * SIDE + y
    return blk * 4 + (z % 2) * 2 + core


def partners(axes, step):
    pairs = []
    for x in range(SIDE):
        for y in range(SIDE):
            for z in range(SIDE):
                for core in range(2):
                    to = {"x": x, "y": y, "z": z}
                    at = to[axes[core]]
                    if step == "both" or (step == "near") == (core == 0):
                        at = at ^ 1
                    if step == "both" or (step == "near") == (core == 1):
                        at = SIDE - 1 - at
                    to[axes[core]] = at
                    pairs.append((place(x, y, z, core), place(to["x"], to["y"], to["z"], core)))
    return pairs


STEPS = {(axes, step): partners(axes, step) for axes in ("xy", "yx", "zz") for step in ("near", "far", "both")}
SWAP = [(d, d ^ 1) for d in range(2 * SIDE**3)]


def move(v, axes, step):
    return lax.ppermute(v, AXES, STEPS[axes, step])


def swap(v):
    return lax.ppermute(v, AXES, SWAP)


def dot_t(a, b):
    return lax.dot_general(a, b, (((1,), (1,)), ((), ())), preferred_element_type=jnp.float32)


def lanes(w):
    rest = -w.shape[1] % 128
    if rest:
        w = jnp.concatenate([w, jnp.zeros((w.shape[0], rest), w.dtype)], axis=1)
    return sum(w[:, k : k + 128] for k in range(0, w.shape[1], 128))


def pair_kernel(counts, n_others, block, span, fresh, last, scale, *refs):
    take = iter(refs)
    n_batch = len(counts)
    rows_refs = [[next(take) for _ in range(count)] for count in counts]
    other_refs = [next(take) for _ in range(n_others)]
    state_in = [None if new else (next(take), next(take)) for new in fresh]
    state_out = [[next(take) for _ in range(count if last else 2)] for count in counts]
    others_b, others_norms = take
    width = rows_refs[0][0].shape[1]
    kappa = math.log2(math.e) / (4.0 * width)

    def norms_of(others):
        norms = jnp.sum(others * others, axis=1, keepdims=True) * kappa
        return jnp.transpose(jnp.broadcast_to(norms, (norms.shape[0], 128)))[:8]

    gens, reals = [], []
    for ref in other_refs:
        for at in range(0, ref.shape[0], block):
            gens.append(ref[at : at + span])
            reals.append(ref[at + span : at + block])
    gens, reals = jnp.concatenate(gens, axis=0), jnp.concatenate(reals, axis=0)
    n_real = reals.shape[0]
    others_norms[:, :n_real] = norms_of(reals)
    others_b[:n_real] = reals.astype(jnp.bfloat16)
    n_gen = gens.shape[0]
    end = n_real + n_gen
    others_norms[:, n_real:] = norms_of(gens)
    high = gens.astype(jnp.bfloat16)
    others_b[n_real:end] = high
    others_b[end : end + n_gen] = (gens - high.astype(jnp.float32)).astype(jnp.bfloat16)
    others_b[end + n_gen :] = high

    for k in range(n_batch):
        rows = jnp.concatenate([r[...] for r in rows_refs[k]], axis=0)
        row_norms = jnp.sum(rows * rows, axis=1, keepdims=True) * kappa
        rows_b = (rows * (2.0 * kappa)).astype(jnp.bfloat16)

        def weights(at, to, factor):
            power = jnp.minimum(dot_t(rows_b, others_b[at:to]) - row_norms - others_norms[:1, at:to], 0.0)
            e = jnp.exp2(power)
            e2 = e * e
            return (0.5 * factor) * e + e2 * (factor + (2.0 * factor) * e2)

        acc, sums = (0.0, 0.0) if fresh[k] else (state_in[k][0][...], state_in[k][1][...])
        w_real, w_gen = weights(0, n_real, -1.0), weights(n_real, end, float(scale))
        sums = sums + lanes(w_real) + lanes(w_gen)
        w_hi = w_gen.astype(jnp.bfloat16)
        w_lo = (w_gen - w_hi.astype(jnp.float32)).astype(jnp.bfloat16)
        w = [w_real.astype(jnp.bfloat16), w_hi, w_hi, w_lo]
        w = jnp.concatenate(w, axis=1)
        acc = acc + jnp.dot(w, others_b[...], preferred_element_type=jnp.float32)
        if last:
            total = jnp.sum(sums, axis=1, keepdims=True)
            out = (total * rows - acc) * last
            at = 0
            for half in state_out[k]:
                half[...] = out[at : at + half.shape[0]]
                at += half.shape[0]
        else:
            state_out[k][0][...] = acc
            state_out[k][1][...] = sums


def pairs(rows, others, block, span, states, last, scale):
    count, width = sum(v.shape[0] for v in rows[0]), rows[0][0].shape[1]
    f32, bf16 = jnp.float32, jnp.bfloat16
    if last:
        shapes = [[jax.ShapeDtypeStruct(v.shape, f32) for v in batch] for batch in rows]
    else:
        shapes = [[jax.ShapeDtypeStruct((count, width), f32), jax.ShapeDtypeStruct((count, 128), f32)] for _ in rows]
    operands = [v for batch in rows for v in batch] + list(others)
    aliases = {}
    for k, state in enumerate(states):
        if state is not None:
            if not last:
                aliases.update({len(operands): 2 * k, len(operands) + 1: 2 * k + 1})
            operands += state
    n_others = sum(v.shape[0] for v in others)
    n_gen = n_others // block * span
    n_real = n_others - n_gen
    scratch = [pltpu.VMEM((n_real + 3 * n_gen, width), bf16), pltpu.VMEM((8, n_real + n_gen), f32)]
    n_pairs = count * len(rows) * (n_real + 2 * n_gen)
    vmem = pl.BlockSpec(memory_space=pltpu.VMEM)
    outs = pl.pallas_call(
        functools.partial(pair_kernel, [len(batch) for batch in rows], len(others), block, span, [s is None for s in states], last, scale),
        out_shape=[v for batch in shapes for v in batch],
        in_specs=[vmem] * len(operands),
        out_specs=[vmem] * sum(len(batch) for batch in shapes),
        scratch_shapes=scratch,
        input_output_aliases=aliases,
        cost_estimate=pl.CostEstimate(
            flops=4 * n_pairs * width, bytes_accessed=4 * width * (n_real + n_gen + 3 * count), transcendentals=n_pairs
        ),
        compiler_params=pltpu.CompilerParams(vmem_limit_bytes=24 * 2**20),
    )(*operands)
    outs = iter(outs)
    return [tuple(next(outs) for _ in batch) for batch in shapes]


def resident(v):
    def copy(v_ref, out_ref):
        out_ref[...] = v_ref[...]

    vmem = pl.BlockSpec(memory_space=pltpu.VMEM)
    return pl.pallas_call(copy, out_shape=jax.ShapeDtypeStruct(v.shape, v.dtype), in_specs=[vmem], out_specs=vmem)(v)


def after(v, *others):
    return lax.optimization_barrier((v, *others))[0]


def resident(v):
    def copy(v_ref, out_ref):
        out_ref[...] = v_ref[...]

    vmem = pl.BlockSpec(memory_space=pltpu.VMEM)
    return pl.pallas_call(copy, out_shape=jax.ShapeDtypeStruct(v.shape, v.dtype), in_specs=[vmem], out_specs=vmem)(v)


def after(v, *others):
    return lax.optimization_barrier((v, *others))[0]


def on_device(generated, real_bank, subset_rows):
    devices = lax.axis_size("blk") * lax.axis_size("rep")
    total_gen = generated.shape[0] * devices
    total_real = subset_rows.shape[0] * devices
    n = generated.shape[0]
    scale = total_real // total_gen

    generated = resident(generated)
    real = real_bank.at[subset_rows].get(mode="promise_in_bounds", wrap_negative_indices=False)
    own = jnp.concatenate([generated, real], axis=0)
    own_two = jnp.concatenate([own, swap(own)], axis=0)
    count = own.shape[0]
    add = functools.partial(pairs, block=count, span=n, scale=scale)
    x_near = move(own_two, "zz", "near")

    line = [generated] + [move(generated, "xy", step) for step in ("near", "far", "both")]
    line = jnp.concatenate(line, axis=0)
    half = 2 * n
    line_near, line_far = move(line, "yx", "near"), move(line, "yx", "far")
    x_near, line_near, line_far = lax.optimization_barrier((x_near, line_near, line_far))
    x_both = move(x_near[:count], "zz", "far")
    x_far = swap(x_near)
    both = [move(line_near[:half], "yx", "far"), move(line_far[half:], "yx", "near")]
    near_two, far_two = (line_near[:half], line_near[half:]), (line_far[:half], line_far[half:])
    rows = [[line], [near_two[0], far_two[1]], [near_two[1], far_two[0]], both]
    s = [None] * SIDE
    s[:3] = add(rows[:3], [own_two], states=s[:3], last=None)
    x_far, _ = lax.optimization_barrier((x_far, s[:3]))
    s[:3] = add(rows[:3], [x_near, x_far], states=s[:3], last=None)
    both, _ = lax.optimization_barrier((both, s[:3]))
    rows[3] = both
    s[3:] = add(rows[3:], [own_two, x_near, x_far], states=s[3:], last=None)
    x_both, _ = lax.optimization_barrier((x_both, s))
    both_swapped = swap(x_both)
    s[2:] = add(rows[2:], [x_both], states=s[2:], last=None)
    both_swapped, _ = lax.optimization_barrier((both_swapped, s))
    near_rest, both = add(rows[2:], [both_swapped], states=s[2:], last=1.0 / total_real)
    near_rest, far_rest = near_rest
    line, near_far = add(rows[:2], [x_both, both_swapped], states=s[:2], last=1.0 / total_real)

    first_near = move(jnp.concatenate([both[1], near_rest], axis=0), "yx", "near")
    first_far = move(jnp.concatenate([both[0], far_rest], axis=0), "yx", "far")
    first_near, first_far = lax.optimization_barrier((first_near, first_far))
    to_near = move(near_far[0] + first_far[:half], "yx", "near")
    to_far = move(near_far[1] + first_near[:half], "yx", "far")
    (line,) = line
    upper = line[:half] + first_far[half:] + to_near
    lower = line[half:] + first_near[half:] + to_far
    out = move(lower[n:], "xy", "both") + move(lower[:n], "xy", "far")
    return upper[:n] + move(upper[n:], "xy", "near") + out


def solution(mesh):
    in_specs = (P(AXES, None), P(AXES, None), P(AXES))
    return jax.shard_map(on_device, mesh=mesh, in_specs=in_specs, out_specs=P(AXES, None), check_vma=False)
```

```python
import functools
import math

import jax
import jax.numpy as jnp
from jax import lax
from jax.experimental import pallas as pl
from jax.experimental.pallas import tpu as pltpu
from jax.sharding import PartitionSpec as P

AXES = ("blk", "rep")
SIDE = 4


def place(x, y, z, core):
    blk = (x * 2 + z // 2) * SIDE + y
    return blk * 4 + (z % 2) * 2 + core


def partners(axes, step):
    pairs = []
    for x in range(SIDE):
        for y in range(SIDE):
            for z in range(SIDE):
                for core in range(2):
                    to = {"x": x, "y": y, "z": z}
                    at = to[axes[core]]
                    if step == "both" or (step == "near") == (core == 0):
                        at = at ^ 1
                    if step == "both" or (step == "near") == (core == 1):
                        at = SIDE - 1 - at
                    to[axes[core]] = at
                    pairs.append((place(x, y, z, core), place(to["x"], to["y"], to["z"], core)))
    return pairs


STEPS = {(axes, step): partners(axes, step) for axes in ("xy", "yx", "zz") for step in ("near", "far", "both")}
SWAP = [(d, d ^ 1) for d in range(2 * SIDE**3)]


def move(v, axes, step):
    return lax.ppermute(v, AXES, STEPS[axes, step])


def swap(v):
    return lax.ppermute(v, AXES, SWAP)


def dot_t(a, b):
    return lax.dot_general(a, b, (((1,), (1,)), ((), ())), preferred_element_type=jnp.float32)


def lanes(w):
    rest = -w.shape[1] % 128
    if rest:
        w = jnp.concatenate([w, jnp.zeros((w.shape[0], rest), w.dtype)], axis=1)
    return sum(w[:, k : k + 128] for k in range(0, w.shape[1], 128))


def pair_kernel(counts, n_others, block, span, fresh, last, scale, *refs):
    take = iter(refs)
    n_batch = len(counts)
    rows_refs = [[next(take) for _ in range(count)] for count in counts]
    other_refs = [next(take) for _ in range(n_others)]
    state_in = [None if new else (next(take), next(take)) for new in fresh]
    state_out = [[next(take) for _ in range(count if last else 2)] for count in counts]
    others_b, others_norms = take
    width = rows_refs[0][0].shape[1]
    kappa = math.log2(math.e) / (4.0 * width)

    def norms_of(others):
        norms = jnp.sum(others * others, axis=1, keepdims=True) * kappa
        return jnp.transpose(jnp.broadcast_to(norms, (norms.shape[0], 128)))[:8]

    gens, reals = [], []
    for ref in other_refs:
        for at in range(0, ref.shape[0], block):
            gens.append(ref[at : at + span])
            reals.append(ref[at + span : at + block])
    gens, reals = jnp.concatenate(gens, axis=0), jnp.concatenate(reals, axis=0)
    n_real = reals.shape[0]
    others_norms[:, :n_real] = norms_of(reals)
    others_b[:n_real] = reals.astype(jnp.bfloat16)
    n_gen = gens.shape[0]
    end = n_real + n_gen
    others_norms[:, n_real:] = norms_of(gens)
    high = gens.astype(jnp.bfloat16)
    others_b[n_real:end] = high
    others_b[end : end + n_gen] = (gens - high.astype(jnp.float32)).astype(jnp.bfloat16)
    others_b[end + n_gen :] = high

    for k in range(n_batch):
        rows = jnp.concatenate([r[...] for r in rows_refs[k]], axis=0)
        row_norms = jnp.sum(rows * rows, axis=1, keepdims=True) * kappa
        rows_b = (rows * (2.0 * kappa)).astype(jnp.bfloat16)

        def weights(at, to, factor):
            power = jnp.minimum(dot_t(rows_b, others_b[at:to]) - row_norms - others_norms[:1, at:to], 0.0)
            e = jnp.exp2(power)
            e2 = e * e
            return (0.5 * factor) * e + e2 * (factor + (2.0 * factor) * e2)

        acc, sums = (0.0, 0.0) if fresh[k] else (state_in[k][0][...], state_in[k][1][...])
        w_real, w_gen = weights(0, n_real, -1.0), weights(n_real, end, float(scale))
        sums = sums + lanes(w_real) + lanes(w_gen)
        w_hi = w_gen.astype(jnp.bfloat16)
        w_lo = (w_gen - w_hi.astype(jnp.float32)).astype(jnp.bfloat16)
        w = [w_real.astype(jnp.bfloat16), w_hi, w_hi, w_lo]
        w = jnp.concatenate(w, axis=1)
        acc = acc + jnp.dot(w, others_b[...], preferred_element_type=jnp.float32)
        if last:
            total = jnp.sum(sums, axis=1, keepdims=True)
            out = (total * rows - acc) * last
            at = 0
            for half in state_out[k]:
                half[...] = out[at : at + half.shape[0]]
                at += half.shape[0]
        else:
            state_out[k][0][...] = acc
            state_out[k][1][...] = sums


def pairs(rows, others, block, span, states, last, scale):
    count, width = sum(v.shape[0] for v in rows[0]), rows[0][0].shape[1]
    f32, bf16 = jnp.float32, jnp.bfloat16
    if last:
        shapes = [[jax.ShapeDtypeStruct(v.shape, f32) for v in batch] for batch in rows]
    else:
        shapes = [[jax.ShapeDtypeStruct((count, width), f32), jax.ShapeDtypeStruct((count, 128), f32)] for _ in rows]
    operands = [v for batch in rows for v in batch] + list(others)
    aliases = {}
    for k, state in enumerate(states):
        if state is not None:
            if not last:
                aliases.update({len(operands): 2 * k, len(operands) + 1: 2 * k + 1})
            operands += state
    n_others = sum(v.shape[0] for v in others)
    n_gen = n_others // block * span
    n_real = n_others - n_gen
    scratch = [pltpu.VMEM((n_real + 3 * n_gen, width), bf16), pltpu.VMEM((8, n_real + n_gen), f32)]
    n_pairs = count * len(rows) * (n_real + 2 * n_gen)
    vmem = pl.BlockSpec(memory_space=pltpu.VMEM)
    outs = pl.pallas_call(
        functools.partial(pair_kernel, [len(batch) for batch in rows], len(others), block, span, [s is None for s in states], last, scale),
        out_shape=[v for batch in shapes for v in batch],
        in_specs=[vmem] * len(operands),
        out_specs=[vmem] * sum(len(batch) for batch in shapes),
        scratch_shapes=scratch,
        input_output_aliases=aliases,
        cost_estimate=pl.CostEstimate(
            flops=4 * n_pairs * width, bytes_accessed=4 * width * (n_real + n_gen + 3 * count), transcendentals=n_pairs
        ),
        compiler_params=pltpu.CompilerParams(vmem_limit_bytes=24 * 2**20),
    )(*operands)
    outs = iter(outs)
    return [tuple(next(outs) for _ in batch) for batch in shapes]


def resident(v):
    def copy(v_ref, out_ref):
        out_ref[...] = v_ref[...]

    vmem = pl.BlockSpec(memory_space=pltpu.VMEM)
    return pl.pallas_call(copy, out_shape=jax.ShapeDtypeStruct(v.shape, v.dtype), in_specs=[vmem], out_specs=vmem)(v)


def after(v, *others):
    return lax.optimization_barrier((v, *others))[0]


def resident(v):
    def copy(v_ref, out_ref):
        out_ref[...] = v_ref[...]

    vmem = pl.BlockSpec(memory_space=pltpu.VMEM)
    return pl.pallas_call(copy, out_shape=jax.ShapeDtypeStruct(v.shape, v.dtype), in_specs=[vmem], out_specs=vmem)(v)


def after(v, *others):
    return lax.optimization_barrier((v, *others))[0]


def on_device(generated, real_bank, subset_rows):
    devices = lax.axis_size("blk") * lax.axis_size("rep")
    total_gen = generated.shape[0] * devices
    total_real = subset_rows.shape[0] * devices
    n = generated.shape[0]
    scale = total_real // total_gen

    generated = resident(generated)
    real = real_bank.at[subset_rows].get(mode="promise_in_bounds", wrap_negative_indices=False)
    own = jnp.concatenate([generated, real], axis=0)
    own_two = jnp.concatenate([own, swap(own)], axis=0)
    count = own.shape[0]
    add = functools.partial(pairs, block=count, span=n, scale=scale)
    x_near = move(own_two, "zz", "near")

    line = [generated] + [move(generated, "xy", step) for step in ("near", "far", "both")]
    line = jnp.concatenate(line, axis=0)
    half = 2 * n
    line_near, line_far = move(line, "yx", "near"), move(line, "yx", "far")
    x_near, line_near, line_far = lax.optimization_barrier((x_near, line_near, line_far))
    x_both = move(x_near[:count], "zz", "far")
    x_far = swap(x_near)
    both = [move(line_near[:half], "yx", "far"), move(line_far[half:], "yx", "near")]
    rows = [[line], [line_near], [line_far], both]
    s = [None] * SIDE
    s[:3] = add(rows[:3], [own_two], states=s[:3], last=None)
    x_far, _ = lax.optimization_barrier((x_far, s[:3]))
    s[:3] = add(rows[:3], [x_near, x_far], states=s[:3], last=None)
    both, _ = lax.optimization_barrier((both, s[:3]))
    rows[3] = both
    s[3:] = add(rows[3:], [own_two, x_near, x_far], states=s[3:], last=None)
    x_both, _ = lax.optimization_barrier((x_both, s))
    both_swapped = swap(x_both)
    s[1:] = add(rows[1:], [x_both], states=s[1:], last=None)
    both_swapped, _ = lax.optimization_barrier((both_swapped, s))
    (both,) = add(rows[3:], [both_swapped], states=s[3:], last=1.0 / total_real)
    s, both = lax.optimization_barrier((s, both))
    (line_near,), (line_far,) = add(rows[1:3], [both_swapped], states=s[1:3], last=1.0 / total_real)
    ((line,),) = add(rows[:1], [x_both, both_swapped], states=s[:1], last=1.0 / total_real)

    add_near, add_far = move(both[0], "yx", "far"), move(both[1], "yx", "near")
    extra = 16
    near_rest = move(line_near[half - extra :], "yx", "near")
    far_rest = move(line_far[: half + extra], "yx", "far")
    add_near, add_far, line = lax.optimization_barrier((add_near, add_far, line))
    to_near = move(line_near[:half] + add_near, "yx", "near")
    to_far = move(line_far[half:] + add_far, "yx", "far")
    line = line + jnp.concatenate([far_rest[:half], near_rest[extra:]], axis=0)
    line, to_near, to_far = lax.optimization_barrier((line, to_near, to_far))
    upper, lower = line[:half] + to_near, line[half:] + to_far
    out = move(lower[n:], "xy", "both") + move(lower[:n], "xy", "far")
    return upper[:n] + move(upper[n:], "xy", "near") + out


def solution(mesh):
    in_specs = (P(AXES, None), P(AXES, None), P(AXES))
    return jax.shard_map(on_device, mesh=mesh, in_specs=in_specs, out_specs=P(AXES, None), check_vma=False)
```

```python
import functools
import math

import jax
import jax.numpy as jnp
from jax import lax
from jax.experimental import pallas as pl
from jax.experimental.pallas import tpu as pltpu
from jax.sharding import PartitionSpec as P

AXES = ("blk", "rep")
SIDE = 4


def place(x, y, z, core):
    blk = (x * 2 + z // 2) * SIDE + y
    return blk * 4 + (z % 2) * 2 + core


def partners(axes, step):
    pairs = []
    for x in range(SIDE):
        for y in range(SIDE):
            for z in range(SIDE):
                for core in range(2):
                    to = {"x": x, "y": y, "z": z}
                    at = to[axes[core]]
                    if step == "both" or (step == "near") == (core == 0):
                        at = at ^ 1
                    if step == "both" or (step == "near") == (core == 1):
                        at = SIDE - 1 - at
                    to[axes[core]] = at
                    pairs.append((place(x, y, z, core), place(to["x"], to["y"], to["z"], core)))
    return pairs


STEPS = {(axes, step): partners(axes, step) for axes in ("xy", "yx", "zz") for step in ("near", "far", "both")}
SWAP = [(d, d ^ 1) for d in range(2 * SIDE**3)]


def move(v, axes, step):
    return lax.ppermute(v, AXES, STEPS[axes, step])


def swap(v):
    return lax.ppermute(v, AXES, SWAP)


def dot_t(a, b):
    return lax.dot_general(a, b, (((1,), (1,)), ((), ())), preferred_element_type=jnp.float32)


def lanes(w):
    rest = -w.shape[1] % 128
    if rest:
        w = jnp.concatenate([w, jnp.zeros((w.shape[0], rest), w.dtype)], axis=1)
    return sum(w[:, k : k + 128] for k in range(0, w.shape[1], 128))


def pair_kernel(counts, n_others, block, span, fresh, last, scale, *refs):
    take = iter(refs)
    n_batch = len(counts)
    rows_refs = [[next(take) for _ in range(count)] for count in counts]
    other_refs = [next(take) for _ in range(n_others)]
    state_in = [None if new else (next(take), next(take)) for new in fresh]
    state_out = [[next(take) for _ in range(count if last else 2)] for count in counts]
    others_b, others_norms = take
    width = rows_refs[0][0].shape[1]
    kappa = math.log2(math.e) / (4.0 * width)

    def norms_of(others):
        norms = jnp.sum(others * others, axis=1, keepdims=True) * kappa
        return jnp.transpose(jnp.broadcast_to(norms, (norms.shape[0], 128)))[:8]

    gens, reals = [], []
    for ref in other_refs:
        for at in range(0, ref.shape[0], block):
            gens.append(ref[at : at + span])
            reals.append(ref[at + span : at + block])
    gens, reals = jnp.concatenate(gens, axis=0), jnp.concatenate(reals, axis=0)
    n_real = reals.shape[0]
    others_norms[:, :n_real] = norms_of(reals)
    others_b[:n_real] = reals.astype(jnp.bfloat16)
    n_gen = gens.shape[0]
    end = n_real + n_gen
    others_norms[:, n_real:] = norms_of(gens)
    high = gens.astype(jnp.bfloat16)
    others_b[n_real:end] = high
    others_b[end : end + n_gen] = (gens - high.astype(jnp.float32)).astype(jnp.bfloat16)
    others_b[end + n_gen :] = high

    for k in range(n_batch):
        rows = jnp.concatenate([r[...] for r in rows_refs[k]], axis=0)
        row_norms = jnp.sum(rows * rows, axis=1, keepdims=True) * kappa
        rows_b = (rows * (2.0 * kappa)).astype(jnp.bfloat16)

        def weights(at, to, factor):
            power = jnp.minimum(dot_t(rows_b, others_b[at:to]) - row_norms - others_norms[:1, at:to], 0.0)
            e = jnp.exp2(power)
            e2 = e * e
            return (0.5 * factor) * e + e2 * (factor + (2.0 * factor) * e2)

        acc, sums = (0.0, 0.0) if fresh[k] else (state_in[k][0][...], state_in[k][1][...])
        w_real, w_gen = weights(0, n_real, -1.0), weights(n_real, end, float(scale))
        sums = sums + lanes(w_real) + lanes(w_gen)
        w_hi = w_gen.astype(jnp.bfloat16)
        w_lo = (w_gen - w_hi.astype(jnp.float32)).astype(jnp.bfloat16)
        w = [w_real.astype(jnp.bfloat16), w_hi, w_hi, w_lo]
        w = jnp.concatenate(w, axis=1)
        acc = acc + jnp.dot(w, others_b[...], preferred_element_type=jnp.float32)
        if last:
            total = jnp.sum(sums, axis=1, keepdims=True)
            out = (total * rows - acc) * last
            at = 0
            for half in state_out[k]:
                half[...] = out[at : at + half.shape[0]]
                at += half.shape[0]
        else:
            state_out[k][0][...] = acc
            state_out[k][1][...] = sums


def pairs(rows, others, block, span, states, last, scale):
    count, width = sum(v.shape[0] for v in rows[0]), rows[0][0].shape[1]
    f32, bf16 = jnp.float32, jnp.bfloat16
    if last:
        shapes = [[jax.ShapeDtypeStruct(v.shape, f32) for v in batch] for batch in rows]
    else:
        shapes = [[jax.ShapeDtypeStruct((count, width), f32), jax.ShapeDtypeStruct((count, 128), f32)] for _ in rows]
    operands = [v for batch in rows for v in batch] + list(others)
    aliases = {}
    for k, state in enumerate(states):
        if state is not None:
            if not last:
                aliases.update({len(operands): 2 * k, len(operands) + 1: 2 * k + 1})
            operands += state
    n_others = sum(v.shape[0] for v in others)
    n_gen = n_others // block * span
    n_real = n_others - n_gen
    scratch = [pltpu.VMEM((n_real + 3 * n_gen, width), bf16), pltpu.VMEM((8, n_real + n_gen), f32)]
    n_pairs = count * len(rows) * (n_real + 2 * n_gen)
    vmem = pl.BlockSpec(memory_space=pltpu.VMEM)
    outs = pl.pallas_call(
        functools.partial(pair_kernel, [len(batch) for batch in rows], len(others), block, span, [s is None for s in states], last, scale),
        out_shape=[v for batch in shapes for v in batch],
        in_specs=[vmem] * len(operands),
        out_specs=[vmem] * sum(len(batch) for batch in shapes),
        scratch_shapes=scratch,
        input_output_aliases=aliases,
        cost_estimate=pl.CostEstimate(
            flops=4 * n_pairs * width, bytes_accessed=4 * width * (n_real + n_gen + 3 * count), transcendentals=n_pairs
        ),
        compiler_params=pltpu.CompilerParams(vmem_limit_bytes=24 * 2**20),
    )(*operands)
    outs = iter(outs)
    return [tuple(next(outs) for _ in batch) for batch in shapes]


def resident(v):
    def copy(v_ref, out_ref):
        out_ref[...] = v_ref[...]

    vmem = pl.BlockSpec(memory_space=pltpu.VMEM)
    return pl.pallas_call(copy, out_shape=jax.ShapeDtypeStruct(v.shape, v.dtype), in_specs=[vmem], out_specs=vmem)(v)


def after(v, *others):
    return lax.optimization_barrier((v, *others))[0]


def resident(v):
    def copy(v_ref, out_ref):
        out_ref[...] = v_ref[...]

    vmem = pl.BlockSpec(memory_space=pltpu.VMEM)
    return pl.pallas_call(copy, out_shape=jax.ShapeDtypeStruct(v.shape, v.dtype), in_specs=[vmem], out_specs=vmem)(v)


def after(v, *others):
    return lax.optimization_barrier((v, *others))[0]


def on_device(generated, real_bank, subset_rows):
    devices = lax.axis_size("blk") * lax.axis_size("rep")
    total_gen = generated.shape[0] * devices
    total_real = subset_rows.shape[0] * devices
    n = generated.shape[0]
    scale = total_real // total_gen

    generated = resident(generated)
    real = real_bank.at[subset_rows].get(mode="promise_in_bounds", wrap_negative_indices=False)
    own = jnp.concatenate([generated, real], axis=0)
    own_swapped = swap(own)
    count = own.shape[0]
    add = functools.partial(pairs, block=count, span=n, scale=scale)
    x_near = move(own, "zz", "near")
    x_far = move(own, "zz", "far")
    x_both = move(x_near, "zz", "far")

    line = [generated] + [move(generated, "xy", step) for step in ("near", "far", "both")]
    line = jnp.concatenate(line, axis=0)
    half = 2 * n
    line_near, line_far = move(line, "yx", "near"), move(line, "yx", "far")
    both = [move(line_near[:half], "yx", "far"), move(line_far[half:], "yx", "near")]
    rows = [[line], [line_near], [line_far], both]
    s = [None] * SIDE
    s[:3] = add(rows[:3], [own, own_swapped], states=s[:3], last=None)
    x_near_swapped = swap(after(x_near, line_near, line_far))
    x_far, x_near_swapped, _ = lax.optimization_barrier((x_far, x_near_swapped, s[:3]))
    cuts = [0, 160, 320]
    x_far_swapped = tuple(swap(x_far[a:b]) for a, b in zip(cuts, cuts[1:]))
    s[:3] = add(rows[:3], [x_near, x_near_swapped], states=s[:3], last=None)
    both, _ = lax.optimization_barrier((both, s[:3]))
    rows[3] = both
    s[3:] = add(rows[3:], [own, own_swapped, x_near, x_near_swapped], states=s[3:], last=None)
    x_far_swapped, _ = lax.optimization_barrier((x_far_swapped, s))
    x_far_swapped = jnp.concatenate(x_far_swapped, axis=0)
    s = add(rows, [x_far, x_far_swapped], states=s, last=None)
    x_both, _ = lax.optimization_barrier((x_both, s))
    both_swapped = swap(x_both)
    s[1:] = add(rows[1:], [x_both], states=s[1:], last=None)
    both_swapped, _ = lax.optimization_barrier((both_swapped, s))
    (both,) = add(rows[3:], [both_swapped], states=s[3:], last=1.0 / total_real)
    s, both = lax.optimization_barrier((s, both))
    (line_near,), (line_far,) = add(rows[1:3], [both_swapped], states=s[1:3], last=1.0 / total_real)
    ((line,),) = add(rows[:1], [x_both, both_swapped], states=s[:1], last=1.0 / total_real)

    add_near, add_far = move(both[0], "yx", "far"), move(both[1], "yx", "near")
    extra = 16
    near_rest = move(line_near[half - extra :], "yx", "near")
    far_rest = move(line_far[: half + extra], "yx", "far")
    add_near, add_far, line = lax.optimization_barrier((add_near, add_far, line))
    to_near = move(line_near[:half] + add_near, "yx", "near")
    to_far = move(line_far[half:] + add_far, "yx", "far")
    line = line + jnp.concatenate([far_rest[:half], near_rest[extra:]], axis=0)
    line, to_near, to_far = lax.optimization_barrier((line, to_near, to_far))
    upper, lower = line[:half] + to_near, line[half:] + to_far
    out = move(lower[n:], "xy", "both") + move(lower[:n], "xy", "far")
    return upper[:n] + move(upper[n:], "xy", "near") + out


def solution(mesh):
    in_specs = (P(AXES, None), P(AXES, None), P(AXES))
    return jax.shard_map(on_device, mesh=mesh, in_specs=in_specs, out_specs=P(AXES, None), check_vma=False)
```

```python
import functools
import math

import jax
import jax.numpy as jnp
from jax import lax
from jax.experimental import pallas as pl
from jax.experimental.pallas import tpu as pltpu
from jax.sharding import PartitionSpec as P

AXES = ("blk", "rep")
SIDE = 4


def place(x, y, z, core):
    blk = (x * 2 + z // 2) * SIDE + y
    return blk * 4 + (z % 2) * 2 + core


def partners(axes, step):
    pairs = []
    for x in range(SIDE):
        for y in range(SIDE):
            for z in range(SIDE):
                for core in range(2):
                    to = {"x": x, "y": y, "z": z}
                    at = to[axes[core]]
                    if step == "both" or (step == "near") == (core == 0):
                        at = at ^ 1
                    if step == "both" or (step == "near") == (core == 1):
                        at = SIDE - 1 - at
                    to[axes[core]] = at
                    pairs.append((place(x, y, z, core), place(to["x"], to["y"], to["z"], core)))
    return pairs


STEPS = {(axes, step): partners(axes, step) for axes in ("xy", "yx", "zz") for step in ("near", "far", "both")}
SWAP = [(d, d ^ 1) for d in range(2 * SIDE**3)]


def move(v, axes, step):
    return lax.ppermute(v, AXES, STEPS[axes, step])


def swap(v):
    return lax.ppermute(v, AXES, SWAP)


def dot_t(a, b):
    return lax.dot_general(a, b, (((1,), (1,)), ((), ())), preferred_element_type=jnp.float32)


def lanes(w):
    rest = -w.shape[1] % 128
    if rest:
        w = jnp.concatenate([w, jnp.zeros((w.shape[0], rest), w.dtype)], axis=1)
    return sum(w[:, k : k + 128] for k in range(0, w.shape[1], 128))


def pair_kernel(counts, n_others, block, span, fresh, last, scale, *refs):
    take = iter(refs)
    n_batch = len(counts)
    rows_refs = [[next(take) for _ in range(count)] for count in counts]
    other_refs = [next(take) for _ in range(n_others)]
    state_in = [None if new else (next(take), next(take)) for new in fresh]
    state_out = [[next(take) for _ in range(count if last else 2)] for count in counts]
    others_b, others_norms = take
    width = rows_refs[0][0].shape[1]
    kappa = math.log2(math.e) / (4.0 * width)

    def norms_of(others):
        norms = jnp.sum(others * others, axis=1, keepdims=True) * kappa
        return jnp.transpose(jnp.broadcast_to(norms, (norms.shape[0], 128)))[:8]

    gens, reals = [], []
    for ref in other_refs:
        for at in range(0, ref.shape[0], block):
            gens.append(ref[at : at + span])
            reals.append(ref[at + span : at + block])
    gens, reals = jnp.concatenate(gens, axis=0), jnp.concatenate(reals, axis=0)
    n_real = reals.shape[0]
    others_norms[:, :n_real] = norms_of(reals)
    others_b[:n_real] = reals.astype(jnp.bfloat16)
    n_gen = gens.shape[0]
    end = n_real + n_gen
    others_norms[:, n_real:] = norms_of(gens)
    high = gens.astype(jnp.bfloat16)
    others_b[n_real:end] = high
    others_b[end : end + n_gen] = (gens - high.astype(jnp.float32)).astype(jnp.bfloat16)
    others_b[end + n_gen :] = high

    for k in range(n_batch):
        rows = jnp.concatenate([r[...] for r in rows_refs[k]], axis=0)
        row_norms = jnp.sum(rows * rows, axis=1, keepdims=True) * kappa
        rows_b = (rows * (2.0 * kappa)).astype(jnp.bfloat16)

        def weights(at, to, factor):
            power = jnp.minimum(dot_t(rows_b, others_b[at:to]) - row_norms - others_norms[:1, at:to], 0.0)
            e = jnp.exp2(power)
            e2 = e * e
            return (0.5 * factor) * e + e2 * (factor + (2.0 * factor) * e2)

        acc, sums = (0.0, 0.0) if fresh[k] else (state_in[k][0][...], state_in[k][1][...])
        w_real, w_gen = weights(0, n_real, -1.0), weights(n_real, end, float(scale))
        sums = sums + lanes(w_real) + lanes(w_gen)
        w_hi = w_gen.astype(jnp.bfloat16)
        w_lo = (w_gen - w_hi.astype(jnp.float32)).astype(jnp.bfloat16)
        w = [w_real.astype(jnp.bfloat16), w_hi, w_hi, w_lo]
        w = jnp.concatenate(w, axis=1)
        acc = acc + jnp.dot(w, others_b[...], preferred_element_type=jnp.float32)
        if last:
            total = jnp.sum(sums, axis=1, keepdims=True)
            out = (total * rows - acc) * last
            at = 0
            for half in state_out[k]:
                half[...] = out[at : at + half.shape[0]]
                at += half.shape[0]
        else:
            state_out[k][0][...] = acc
            state_out[k][1][...] = sums


def pairs(rows, others, block, span, states, last, scale):
    count, width = sum(v.shape[0] for v in rows[0]), rows[0][0].shape[1]
    f32, bf16 = jnp.float32, jnp.bfloat16
    if last:
        shapes = [[jax.ShapeDtypeStruct(v.shape, f32) for v in batch] for batch in rows]
    else:
        shapes = [[jax.ShapeDtypeStruct((count, width), f32), jax.ShapeDtypeStruct((count, 128), f32)] for _ in rows]
    operands = [v for batch in rows for v in batch] + list(others)
    aliases = {}
    for k, state in enumerate(states):
        if state is not None:
            if not last:
                aliases.update({len(operands): 2 * k, len(operands) + 1: 2 * k + 1})
            operands += state
    n_others = sum(v.shape[0] for v in others)
    n_gen = n_others // block * span
    n_real = n_others - n_gen
    scratch = [pltpu.VMEM((n_real + 3 * n_gen, width), bf16), pltpu.VMEM((8, n_real + n_gen), f32)]
    n_pairs = count * len(rows) * (n_real + 2 * n_gen)
    vmem = pl.BlockSpec(memory_space=pltpu.VMEM)
    outs = pl.pallas_call(
        functools.partial(pair_kernel, [len(batch) for batch in rows], len(others), block, span, [s is None for s in states], last, scale),
        out_shape=[v for batch in shapes for v in batch],
        in_specs=[vmem] * len(operands),
        out_specs=[vmem] * sum(len(batch) for batch in shapes),
        scratch_shapes=scratch,
        input_output_aliases=aliases,
        cost_estimate=pl.CostEstimate(
            flops=4 * n_pairs * width, bytes_accessed=4 * width * (n_real + n_gen + 3 * count), transcendentals=n_pairs
        ),
        compiler_params=pltpu.CompilerParams(vmem_limit_bytes=24 * 2**20),
    )(*operands)
    outs = iter(outs)
    return [tuple(next(outs) for _ in batch) for batch in shapes]


def resident(v):
    def copy(v_ref, out_ref):
        out_ref[...] = v_ref[...]

    vmem = pl.BlockSpec(memory_space=pltpu.VMEM)
    return pl.pallas_call(copy, out_shape=jax.ShapeDtypeStruct(v.shape, v.dtype), in_specs=[vmem], out_specs=vmem)(v)


def after(v, *others):
    return lax.optimization_barrier((v, *others))[0]


def resident(v):
    def copy(v_ref, out_ref):
        out_ref[...] = v_ref[...]

    vmem = pl.BlockSpec(memory_space=pltpu.VMEM)
    return pl.pallas_call(copy, out_shape=jax.ShapeDtypeStruct(v.shape, v.dtype), in_specs=[vmem], out_specs=vmem)(v)


def after(v, *others):
    return lax.optimization_barrier((v, *others))[0]


def on_device(generated, real_bank, subset_rows):
    devices = lax.axis_size("blk") * lax.axis_size("rep")
    total_gen = generated.shape[0] * devices
    total_real = subset_rows.shape[0] * devices
    n = generated.shape[0]
    scale = total_real // total_gen

    generated = resident(generated)
    real = real_bank.at[subset_rows].get(mode="promise_in_bounds", wrap_negative_indices=False)
    own = jnp.concatenate([generated, real], axis=0)
    own_swapped = swap(own)
    count = own.shape[0]
    add = functools.partial(pairs, block=count, span=n, scale=scale)
    x_near = move(own, "zz", "near")
    x_far = move(own, "zz", "far")
    x_both = move(x_near, "zz", "far")

    line = [generated] + [move(generated, "xy", step) for step in ("near", "far", "both")]
    line = jnp.concatenate(line, axis=0)
    half = 2 * n
    line_near, line_far = move(line, "yx", "near"), move(line, "yx", "far")
    both = [move(line_near[:half], "yx", "far"), move(line_far[half:], "yx", "near")]
    rows = [[line], [line_near], [line_far], both]
    s = [None] * SIDE
    s[:3] = add(rows[:3], [own, own_swapped], states=s[:3], last=None)
    x_near_swapped = swap(after(x_near, line_near, line_far))
    x_far, x_near_swapped, _ = lax.optimization_barrier((x_far, x_near_swapped, s[:3]))
    cuts = [0, 160, 320]
    x_far_swapped = tuple(swap(x_far[a:b]) for a, b in zip(cuts, cuts[1:]))
    s[:3] = add(rows[:3], [x_near, x_near_swapped], states=s[:3], last=None)
    both, _ = lax.optimization_barrier((both, s[:3]))
    rows[3] = both
    s[3:] = add(rows[3:], [own, own_swapped, x_near, x_near_swapped], states=s[3:], last=None)
    x_far_swapped, _ = lax.optimization_barrier((x_far_swapped, s))
    x_far_swapped = jnp.concatenate(x_far_swapped, axis=0)
    s[1:] = add(rows[1:], [x_far, x_far_swapped], states=s[1:], last=None)
    x_both, _ = lax.optimization_barrier((x_both, s))
    both_swapped = swap(x_both)
    s[1:] = add(rows[1:], [x_both], states=s[1:], last=None)
    both_swapped, _ = lax.optimization_barrier((both_swapped, s))
    (both,) = add(rows[3:], [both_swapped], states=s[3:], last=1.0 / total_real)
    s, both = lax.optimization_barrier((s, both))
    (line_near,), (line_far,) = add(rows[1:3], [both_swapped], states=s[1:3], last=1.0 / total_real)
    ((line,),) = add(rows[:1], [x_far, x_far_swapped, x_both, both_swapped], states=s[:1], last=1.0 / total_real)

    add_near, add_far = move(both[0], "yx", "far"), move(both[1], "yx", "near")
    extra = 8
    near_rest = move(line_near[half - extra :], "yx", "near")
    far_rest = move(line_far[: half + extra], "yx", "far")
    add_near, add_far, line = lax.optimization_barrier((add_near, add_far, line))
    to_near = move(line_near[:half] + add_near, "yx", "near")
    to_far = move(line_far[half:] + add_far, "yx", "far")
    line = line + jnp.concatenate([far_rest[:half], near_rest[extra:]], axis=0)
    line, to_near, to_far = lax.optimization_barrier((line, to_near, to_far))
    upper, lower = line[:half] + to_near, line[half:] + to_far
    out = move(lower[n:], "xy", "both") + move(lower[:n], "xy", "far")
    return upper[:n] + move(upper[n:], "xy", "near") + out


def solution(mesh):
    in_specs = (P(AXES, None), P(AXES, None), P(AXES))
    return jax.shard_map(on_device, mesh=mesh, in_specs=in_specs, out_specs=P(AXES, None), check_vma=False)
```

```python
import functools
import math

import jax
import jax.numpy as jnp
from jax import lax
from jax.experimental import pallas as pl
from jax.experimental.pallas import tpu as pltpu
from jax.sharding import PartitionSpec as P

AXES = ("blk", "rep")
SIDE = 4


def place(x, y, z, core):
    blk = (x * 2 + z // 2) * SIDE + y
    return blk * 4 + (z % 2) * 2 + core


def partners(axes, step):
    pairs = []
    for x in range(SIDE):
        for y in range(SIDE):
            for z in range(SIDE):
                for core in range(2):
                    to = {"x": x, "y": y, "z": z}
                    at = to[axes[core]]
                    if step == "both" or (step == "near") == (core == 0):
                        at = at ^ 1
                    if step == "both" or (step == "near") == (core == 1):
                        at = SIDE - 1 - at
                    to[axes[core]] = at
                    pairs.append((place(x, y, z, core), place(to["x"], to["y"], to["z"], core)))
    return pairs


STEPS = {(axes, step): partners(axes, step) for axes in ("xy", "yx", "zz") for step in ("near", "far", "both")}
SWAP = [(d, d ^ 1) for d in range(2 * SIDE**3)]


def move(v, axes, step):
    return lax.ppermute(v, AXES, STEPS[axes, step])


def swap(v):
    return lax.ppermute(v, AXES, SWAP)


def dot_t(a, b):
    return lax.dot_general(a, b, (((1,), (1,)), ((), ())), preferred_element_type=jnp.float32)


def lanes(w):
    rest = -w.shape[1] % 128
    if rest:
        w = jnp.concatenate([w, jnp.zeros((w.shape[0], rest), w.dtype)], axis=1)
    return sum(w[:, k : k + 128] for k in range(0, w.shape[1], 128))


def pair_kernel(counts, n_others, block, span, fresh, last, scale, *refs):
    take = iter(refs)
    n_batch = len(counts)
    rows_refs = [[next(take) for _ in range(count)] for count in counts]
    other_refs = [next(take) for _ in range(n_others)]
    state_in = [None if new else (next(take), next(take)) for new in fresh]
    state_out = [[next(take) for _ in range(count if last else 2)] for count in counts]
    others_b, others_norms = take
    width = rows_refs[0][0].shape[1]
    kappa = math.log2(math.e) / (4.0 * width)

    def norms_of(others):
        norms = jnp.sum(others * others, axis=1, keepdims=True) * kappa
        return jnp.transpose(jnp.broadcast_to(norms, (norms.shape[0], 128)))[:8]

    gens, reals = [], []
    for ref in other_refs:
        for at in range(0, ref.shape[0], block):
            gens.append(ref[at : at + span])
            reals.append(ref[at + span : at + block])
    gens, reals = jnp.concatenate(gens, axis=0), jnp.concatenate(reals, axis=0)
    n_real = reals.shape[0]
    others_norms[:, :n_real] = norms_of(reals)
    others_b[:n_real] = reals.astype(jnp.bfloat16)
    n_gen = gens.shape[0]
    end = n_real + n_gen
    others_norms[:, n_real:] = norms_of(gens)
    high = gens.astype(jnp.bfloat16)
    others_b[n_real:end] = high
    others_b[end : end + n_gen] = (gens - high.astype(jnp.float32)).astype(jnp.bfloat16)
    others_b[end + n_gen :] = high

    for k in range(n_batch):
        rows = jnp.concatenate([r[...] for r in rows_refs[k]], axis=0)
        row_norms = jnp.sum(rows * rows, axis=1, keepdims=True) * kappa
        rows_b = (rows * (2.0 * kappa)).astype(jnp.bfloat16)

        def weights(at, to, factor):
            power = jnp.minimum(dot_t(rows_b, others_b[at:to]) - row_norms - others_norms[:1, at:to], 0.0)
            e = jnp.exp2(power)
            e2 = e * e
            return (0.5 * factor) * e + e2 * (factor + (2.0 * factor) * e2)

        acc, sums = (0.0, 0.0) if fresh[k] else (state_in[k][0][...], state_in[k][1][...])
        w_real, w_gen = weights(0, n_real, -1.0), weights(n_real, end, float(scale))
        sums = sums + lanes(w_real) + lanes(w_gen)
        w_hi = w_gen.astype(jnp.bfloat16)
        w_lo = (w_gen - w_hi.astype(jnp.float32)).astype(jnp.bfloat16)
        w = [w_real.astype(jnp.bfloat16), w_hi, w_hi, w_lo]
        w = jnp.concatenate(w, axis=1)
        acc = acc + jnp.dot(w, others_b[...], preferred_element_type=jnp.float32)
        if last:
            total = jnp.sum(sums, axis=1, keepdims=True)
            out = (total * rows - acc) * last
            at = 0
            for half in state_out[k]:
                half[...] = out[at : at + half.shape[0]]
                at += half.shape[0]
        else:
            state_out[k][0][...] = acc
            state_out[k][1][...] = sums


def pairs(rows, others, block, span, states, last, scale):
    count, width = sum(v.shape[0] for v in rows[0]), rows[0][0].shape[1]
    f32, bf16 = jnp.float32, jnp.bfloat16
    if last:
        shapes = [[jax.ShapeDtypeStruct(v.shape, f32) for v in batch] for batch in rows]
    else:
        shapes = [[jax.ShapeDtypeStruct((count, width), f32), jax.ShapeDtypeStruct((count, 128), f32)] for _ in rows]
    operands = [v for batch in rows for v in batch] + list(others)
    aliases = {}
    for k, state in enumerate(states):
        if state is not None:
            if not last:
                aliases.update({len(operands): 2 * k, len(operands) + 1: 2 * k + 1})
            operands += state
    n_others = sum(v.shape[0] for v in others)
    n_gen = n_others // block * span
    n_real = n_others - n_gen
    scratch = [pltpu.VMEM((n_real + 3 * n_gen, width), bf16), pltpu.VMEM((8, n_real + n_gen), f32)]
    n_pairs = count * len(rows) * (n_real + 2 * n_gen)
    vmem = pl.BlockSpec(memory_space=pltpu.VMEM)
    outs = pl.pallas_call(
        functools.partial(pair_kernel, [len(batch) for batch in rows], len(others), block, span, [s is None for s in states], last, scale),
        out_shape=[v for batch in shapes for v in batch],
        in_specs=[vmem] * len(operands),
        out_specs=[vmem] * sum(len(batch) for batch in shapes),
        scratch_shapes=scratch,
        input_output_aliases=aliases,
        cost_estimate=pl.CostEstimate(
            flops=4 * n_pairs * width, bytes_accessed=4 * width * (n_real + n_gen + 3 * count), transcendentals=n_pairs
        ),
        compiler_params=pltpu.CompilerParams(vmem_limit_bytes=24 * 2**20),
    )(*operands)
    outs = iter(outs)
    return [tuple(next(outs) for _ in batch) for batch in shapes]


def resident(v):
    def copy(v_ref, out_ref):
        out_ref[...] = v_ref[...]

    vmem = pl.BlockSpec(memory_space=pltpu.VMEM)
    return pl.pallas_call(copy, out_shape=jax.ShapeDtypeStruct(v.shape, v.dtype), in_specs=[vmem], out_specs=vmem)(v)


def after(v, *others):
    return lax.optimization_barrier((v, *others))[0]


def resident(v):
    def copy(v_ref, out_ref):
        out_ref[...] = v_ref[...]

    vmem = pl.BlockSpec(memory_space=pltpu.VMEM)
    return pl.pallas_call(copy, out_shape=jax.ShapeDtypeStruct(v.shape, v.dtype), in_specs=[vmem], out_specs=vmem)(v)


def after(v, *others):
    return lax.optimization_barrier((v, *others))[0]


def on_device(generated, real_bank, subset_rows):
    devices = lax.axis_size("blk") * lax.axis_size("rep")
    total_gen = generated.shape[0] * devices
    total_real = subset_rows.shape[0] * devices
    n = generated.shape[0]
    scale = total_real // total_gen

    first = generated
    generated = resident(generated)
    real = real_bank.at[subset_rows].get(mode="promise_in_bounds", wrap_negative_indices=False)
    own = jnp.concatenate([generated, real], axis=0)
    own_swapped = swap(own)
    count = own.shape[0]
    add = functools.partial(pairs, block=count, span=n, scale=scale)
    x_near = move(own, "zz", "near")
    x_far = move(own, "zz", "far")
    x_both = move(x_near, "zz", "far")

    line = [generated] + [move(first, "xy", step) for step in ("near", "far", "both")]
    line = jnp.concatenate(line, axis=0)
    half = 2 * n
    line_near, line_far = move(line, "yx", "near"), move(line, "yx", "far")
    both = [move(line_near[:half], "yx", "far"), move(line_far[half:], "yx", "near")]
    rows = [[line], [line_near], [line_far], both]
    s = [None] * SIDE
    s[:3] = add(rows[:3], [own, own_swapped], states=s[:3], last=None)
    x_near_swapped = swap(after(x_near, line_near, line_far))
    x_far, x_near_swapped, _ = lax.optimization_barrier((x_far, x_near_swapped, s[:3]))
    cuts = [0, 160, 320]
    x_far_swapped = tuple(swap(x_far[a:b]) for a, b in zip(cuts, cuts[1:]))
    s[:3] = add(rows[:3], [x_near, x_near_swapped], states=s[:3], last=None)
    both, _ = lax.optimization_barrier((both, s[:3]))
    rows[3] = both
    s[3:] = add(rows[3:], [own, own_swapped, x_near, x_near_swapped], states=s[3:], last=None)
    x_far_swapped, _ = lax.optimization_barrier((x_far_swapped, s))
    x_far_swapped = jnp.concatenate(x_far_swapped, axis=0)
    s[1:] = add(rows[1:], [x_far, x_far_swapped], states=s[1:], last=None)
    x_both, _ = lax.optimization_barrier((x_both, s))
    both_swapped = swap(x_both)
    s[1:] = add(rows[1:], [x_both], states=s[1:], last=None)
    both_swapped, _ = lax.optimization_barrier((both_swapped, s))
    (both,) = add(rows[3:], [both_swapped], states=s[3:], last=1.0 / total_real)
    s, both = lax.optimization_barrier((s, both))
    (line_near,), (line_far,) = add(rows[1:3], [both_swapped], states=s[1:3], last=1.0 / total_real)
    ((line,),) = add(rows[:1], [x_far, x_far_swapped, x_both, both_swapped], states=s[:1], last=1.0 / total_real)

    add_near, add_far = move(both[0], "yx", "far"), move(both[1], "yx", "near")
    extra = 8
    near_rest = move(line_near[half - extra :], "yx", "near")
    far_rest = move(line_far[: half + extra], "yx", "far")
    add_near, add_far, line = lax.optimization_barrier((add_near, add_far, line))
    to_near = move(line_near[:half] + add_near, "yx", "near")
    to_far = move(line_far[half:] + add_far, "yx", "far")
    line = line + jnp.concatenate([far_rest[:half], near_rest[extra:]], axis=0)
    line, to_near, to_far = lax.optimization_barrier((line, to_near, to_far))
    upper, lower = line[:half] + to_near, line[half:] + to_far
    out = move(lower[n:], "xy", "both") + move(lower[:n], "xy", "far")
    return upper[:n] + move(upper[n:], "xy", "near") + out


def solution(mesh):
    in_specs = (P(AXES, None), P(AXES, None), P(AXES))
    return jax.shard_map(on_device, mesh=mesh, in_specs=in_specs, out_specs=P(AXES, None), check_vma=False)
```
